32 devices in a mesh: groups: 2 (over x), replica: 16 (over z, y, core).
Axes of the slice: x: 2, y: 2, z: 4, core: 2. Of those that a mesh axis runs over, the one named last changes fastest.
Arguments:
- page_table: int32 [32, 64], P(('groups', 'replica')), parts along dimension 0, may hold values from 0 to 1023, as said below
- prefix_len: int32 [32], P(('groups', 'replica')), parts along dimension 0, may hold values from 64 to 512, as said below
- page_store: bfloat16 [2048, 8, 2048], P(('groups', 'replica')), parts along dimension 0, may hold values from -16 to 16
- cand_query: bfloat16 [32, 800, 2048], P(('groups', 'replica')), parts along dimension 0, may hold values from -16 to 16
- cand_kv: bfloat16 [32, 800, 2048], P(('groups', 'replica')), parts along dimension 0, may hold values from -6 to 6
Outputs:
- attended: bfloat16 [32, 800, 2048], P(('groups', 'replica')), parts along dimension 0
The draws below stay inside these ranges and needn't reach their ends.
There are 2 independent parts, one for each index of `groups`. The reference program is written for one: setup_inputs(seed, part) draws one part's arguments, and reference() takes and returns one part's arrays. A program takes and returns all parts, laid end to end along the dimension named above; each array names one. Nothing has to cross between parts.
Inputs may be any that keep to these rules, and one draw needn't show every extreme that they name: `page_table`: entry [q, k] = 64 * d + s names slot s of device d, which holds page k of query q's prefix. Every slot is named exactly once. No device holds more than 16 pages of one query, and every query has exactly 16 pages on some device. `prefix_len`: positions from the prefix length on are unused. Some query has 64 tokens and some has 512.
All inputs are finite; a program needn't handle non-finite values.
Results may differ from the reference program's by a relative error of at most 0.007.
Values may be sent and summed in bfloat16 or wider, within the bound.
A program may use at most 128 MiB of HBM per device.

```python
import jax
import jax.numpy as jnp
from jax import lax

HD = 256
QH = 8
KH = 4
PAGE = 8
NP = 64
PLEN = 512
CLEN = 200
CAND = 4
ROWS = 800
QRY = 16
CAP = 16


def draw_page_table(key, part):
    key = jax.random.fold_in(key, 3)
    key_pattern, key_order, key_slots = jax.random.split(key, 3)
    unit = max(1, CAP // 4)
    full_count = NP // (2 * CAP)
    small_count = NP // (2 * unit)
    places = jnp.arange(QRY)
    base = jnp.where(places < full_count, CAP, jnp.where(places < full_count + small_count, unit, 0))
    pattern = base[jax.random.permutation(key_pattern, QRY)].astype(jnp.int32)
    bounds = jnp.cumsum(pattern)
    order = jax.vmap(lambda single: jax.random.permutation(single, NP))(jax.random.split(key_order, QRY))
    slots = jax.vmap(lambda single: jax.random.permutation(single, NP))(jax.random.split(key_slots, QRY))
    offset = jnp.sum((bounds[None, None, :] <= order[:, :, None]).astype(jnp.int32), axis=-1)
    device = (jnp.arange(QRY)[:, None] + offset) % QRY
    return (device * NP + slots[device, order]).astype(jnp.int32)


def draw_prefix_len(key, part):
    key = jax.random.fold_in(key, 5)
    key_lengths, key_first, key_second = jax.random.split(key, 3)
    lengths = jax.random.randint(key_lengths, (QRY,), PLEN // 8, PLEN + 1)
    first_pick = jax.random.randint(key_first, (), 0, QRY)
    second_pick = (first_pick + 1 + jax.random.randint(key_second, (), 0, QRY - 1)) % QRY
    places = jnp.arange(QRY)
    lengths = jnp.where(places == first_pick, PLEN, lengths)
    lengths = jnp.where(places == second_pick, PLEN // 8, lengths)
    return lengths.astype(jnp.int32)


def draw_page_store(key, part):
    key = jax.random.fold_in(key, 11)
    key_base = jax.random.fold_in(key, 0)
    shape = (QRY * NP, PAGE, 2 * KH * HD)
    base = jnp.clip(jax.random.normal(key_base, shape, jnp.float32), -6.0, 6.0)
    return base.astype(jnp.bfloat16)


def draw_cand_query(key, part):
    key = jax.random.fold_in(key, 7)
    key_base = jax.random.fold_in(key, 0)
    shape = (QRY, CAND * CLEN, QH * HD)
    base = jnp.clip(jax.random.normal(key_base, shape, jnp.float32), -6.0, 6.0)
    return base.astype(jnp.bfloat16)


def shard_levels(own_key, extent, shards, smallest, largest):
    def one(position, blocks):
        draws = jax.random.uniform(jax.random.fold_in(jax.random.fold_in(own_key, 6), position), (blocks,), jnp.float32, smallest / len(shards), largest / len(shards))
        return jnp.repeat(jnp.exp(draws), extent[position] // blocks).reshape((-1,) + (1,) * (len(extent) - position - 1))

    gain = one(*shards[0])
    for cut in shards[1:]:
        gain = gain * one(*cut)
    return gain


def centred(stream_key, dims, spread, bound, cuts=(), held_as=jnp.bfloat16):
    array = jax.random.normal(stream_key, dims, jnp.float32) * spread
    if len(cuts) > 0:
        array = shard_levels(stream_key, dims, cuts, -0.22, 0.18) * array
    return jnp.clip(array, min=-bound, max=bound).astype(held_as)


def setup_inputs(seed: int = 0, part: int = 0) -> dict:
    key_of = jax.random.split(jax.random.key(seed), 6)
    part_splits = jax.random.split(jax.random.fold_in(key_of[5], part), 6)
    page_table = draw_page_table(jax.random.fold_in(jax.random.fold_in(key_of[5], part), 71), part)
    prefix_len = draw_prefix_len(jax.random.fold_in(jax.random.fold_in(key_of[5], part), 71), part)
    page_store = draw_page_store(jax.random.fold_in(jax.random.fold_in(key_of[5], part), 71), part)
    cand_query = draw_cand_query(jax.random.fold_in(jax.random.fold_in(key_of[5], part), 71), part)
    cand_kv = centred(part_splits[4], (QRY, ROWS, 2 * KH * HD), 1.0, 6.0, ((0, 16),))
    return dict(page_table=page_table, prefix_len=prefix_len, page_store=page_store, cand_query=cand_query, cand_kv=cand_kv)


def rope_turn(values, positions):
    head_width = values.shape[-1]
    half_width = head_width // 2
    pair_index = jnp.arange(half_width, dtype=jnp.float32)
    inverse = jnp.power(jnp.float32(10000.0), pair_index * (-2.0 / head_width))
    angles = positions.astype(jnp.float32)[:, None] * inverse[None, :]
    cosine = jnp.cos(angles)[:, None, :]
    sine_table = jnp.sin(angles)[:, None, :]
    leading = values[..., :half_width]
    trailing = values[..., half_width:]
    return jnp.concatenate([leading * cosine - trailing * sine_table, trailing * cosine + leading * sine_table], axis=-1)


def attend(rotated, prefix_keys, prefix_values, own_keys, own_values, length):
    scale = HD ** -0.5
    grouped = rotated.astype(jnp.float32).reshape(CAND, CLEN, KH, QH // KH, HD)
    prefix_scores = jnp.einsum("ctkgd,pkd->ctkgp", grouped, prefix_keys.astype(jnp.float32)) * scale
    prefix_scores = 50.0 * jnp.tanh(prefix_scores / 50.0)
    live = jnp.arange(PLEN) < length
    own_grouped = own_keys.astype(jnp.float32).reshape(CAND, CLEN, KH, HD)
    own_scores = jnp.einsum("ctkgd,cskd->ctkgs", grouped, own_grouped) * scale
    own_scores = 50.0 * jnp.tanh(own_scores / 50.0)
    causal = jnp.arange(CLEN)[:, None] >= jnp.arange(CLEN)[None, :]
    prefix_exp = jnp.where(live, jnp.exp(prefix_scores), 0.0)
    own_exp = jnp.where(causal[None, :, None, None, :], jnp.exp(own_scores), 0.0)
    denominator = jnp.sum(prefix_exp, axis=-1) + jnp.sum(own_exp, axis=-1)
    prefix_weights = lax.optimization_barrier(prefix_exp.astype(jnp.bfloat16)).astype(jnp.float32)
    own_weights = lax.optimization_barrier(own_exp.astype(jnp.bfloat16)).astype(jnp.float32)
    own_vals = own_values.astype(jnp.float32).reshape(CAND, CLEN, KH, HD)
    total = jnp.einsum("ctkgp,pkd->ctkgd", prefix_weights, prefix_values.astype(jnp.float32))
    total = total + jnp.einsum("ctkgs,cskd->ctkgd", own_weights, own_vals)
    result = total / denominator[..., None]
    return result.reshape(CAND * CLEN, QH * HD).astype(jnp.bfloat16)


def reference(page_table, prefix_len, page_store, cand_query, cand_kv):
    def one_query(items):
        table, length, queries, paired = items
        pages = page_store[table]
        prefix = pages.reshape(PLEN, 2, KH, HD)
        positions = length + jnp.arange(CAND * CLEN, dtype=jnp.int32) % CLEN
        rotated = rope_turn(queries.astype(jnp.float32).reshape(CAND * CLEN, QH, HD), positions)
        rotated = lax.optimization_barrier(rotated.astype(jnp.bfloat16))
        own = paired.reshape(CAND * CLEN, 2, KH, HD)
        own_keys = rope_turn(own[:, 0].astype(jnp.float32), positions)
        own_keys = lax.optimization_barrier(own_keys.astype(jnp.bfloat16))
        return attend(rotated, prefix[:, 0], prefix[:, 1], own_keys, own[:, 1], length)

    return lax.map(one_query, (page_table, prefix_len, cand_query, cand_kv))
```

```python
import functools
import math

import jax
import jax.numpy as jnp
from jax import lax
from jax.experimental import pallas as pl
from jax.experimental.pallas import tpu as pltpu
from jax.sharding import PartitionSpec as P

HD = 256
QH = 8
KH = 4
CLEN = 200
LANES = 128
MESH = pl.DeviceIdType.MESH


def pick_slots(tables, chosen, capacity, held):
    counted = jnp.cumsum(chosen.astype(jnp.int32), axis=1) - 1
    picked = chosen[:, None, :] & (counted[:, None, :] == jnp.arange(capacity)[None, :, None])
    return jnp.sum(jnp.where(picked, (tables % held)[:, None, :], 0), axis=2)


def padded_exchange(page_table, page_store):
    peers = lax.axis_size("replica")
    my_index = lax.axis_index("replica")
    held = page_store.shape[0]
    capacity = max(2, 4 * held // peers)
    table = page_table[0]
    source = (table // held) % peers
    page_ids = jnp.arange(held)
    same_source = (source[:, None] == source[None, :]) & (page_ids[None, :] < page_ids[:, None])
    rank_here = jnp.sum(same_source.astype(jnp.int32), axis=1)
    every_table = lax.all_gather(page_table, "replica", axis=0, tiled=True)
    mine = (every_table // held) % peers == my_index
    send_slot = pick_slots(every_table, mine, capacity, held)
    outgoing = page_store[send_slot]
    arrived = lax.all_to_all(outgoing, "replica", split_axis=0, concat_axis=0, tiled=True)
    return arrived[source, rank_here].reshape(held * page_store.shape[1], page_store.shape[2])


def route_kernel(groups, peers, held, share, table_ref, out_ref, tables, send_sem, recv_sem):
    group = lax.axis_index("groups")
    me = lax.axis_index("replica")
    total = groups * peers
    flat = group * peers + me
    barrier = pltpu.get_barrier_semaphore()

    def where_is(step):
        other = lax.rem(flat + step, total)
        return other, (lax.div(other, peers), lax.rem(other, peers))

    def greet(step, carry):
        pl.semaphore_signal(barrier, inc=1, device_id=where_is(step)[1], device_id_type=MESH)
        return carry

    lax.fori_loop(1, total, greet, 0)
    tables[pl.ds(flat, 1)] = table_ref[...][None]
    pl.semaphore_wait(barrier, total - 1)

    def outgoing(step):
        return pltpu.make_async_remote_copy(
            src_ref=table_ref,
            dst_ref=tables.at[flat],
            send_sem=send_sem.at[step],
            recv_sem=recv_sem.at[flat],
            device_id=where_is(step)[1],
            device_id_type=MESH,
        )

    def send(step, carry):
        outgoing(step).start()
        return carry

    def finish(step, carry):
        other, place = where_is(step)
        pltpu.make_async_remote_copy(
            src_ref=table_ref,
            dst_ref=tables.at[other],
            send_sem=send_sem.at[step],
            recv_sem=recv_sem.at[other],
            device_id=place,
            device_id_type=MESH,
        ).wait()
        return carry

    lax.fori_loop(1, total, send, 0)
    lax.fori_loop(1, total, finish, 0)

    every = tables[:, 0, :]
    shape = (total, LANES)
    row = lax.broadcasted_iota(jnp.int32, shape, 0)
    lane = lax.broadcasted_iota(jnp.int32, shape, 1)
    valid = lane < held
    query = lax.rem(row, peers)
    owner = jnp.where(valid, lax.rem(lax.div(every, held), peers), -1)
    slot = lax.rem(every, held)
    before = (
        lax.broadcasted_iota(jnp.int32, (LANES, LANES), 0)
        < lax.broadcasted_iota(jnp.int32, (LANES, LANES), 1)
    ).astype(jnp.float32)
    left = lax.broadcasted_iota(jnp.int32, (total, total), 0)
    right = lax.broadcasted_iota(jnp.int32, (total, total), 1)
    together = lax.div(left, peers) == lax.div(right, peers)
    rank = jnp.zeros(shape, jnp.float32)
    for device in range(peers):
        here = (owner == device).astype(jnp.float32)
        along = jnp.dot(here, before, preferred_element_type=jnp.float32)
        nearer = lax.rem(right + (peers - device), peers) < lax.rem(left + (peers - device), peers)
        earlier = (together & nearer).astype(jnp.float32)
        above = jnp.dot(earlier, here, preferred_element_type=jnp.float32)
        above = jnp.sum(above, axis=1, keepdims=True)
        rank = rank + here * (along + above)
    rank = rank.astype(jnp.int32)
    middle = jnp.where(valid, lax.rem(rank, peers), -1)
    layer = lax.div(rank, peers)
    place = jnp.zeros(shape, jnp.float32)
    for device in range(peers):
        here = (middle == device).astype(jnp.float32)
        along = jnp.dot(here, before, preferred_element_type=jnp.float32)
        place = place + here * along
    most = jnp.max(jnp.max(place, axis=1, keepdims=True), axis=0, keepdims=True)
    place = place.astype(jnp.int32)

    mine = lax.div(row, peers) == group
    first_key = jnp.where(mine & (owner == me), middle * share + layer, -1)
    second_key = jnp.where(mine & (middle == me), query * share + place, -1)
    second_value = owner * share + layer
    spots = lax.broadcasted_iota(jnp.int32, (held, LANES), 0)
    first = jnp.zeros((held, LANES), jnp.int32)
    second = jnp.zeros((held, LANES), jnp.int32)
    for index in range(total):
        cut = slice(index, index + 1)
        first = first + jnp.where(spots == first_key[cut], slot[cut], 0)
        second = second + jnp.where(spots == second_key[cut], second_value[cut], 0)
    ones = jnp.ones((8, LANES), jnp.float32)
    turn = (((1,), (1,)), ((), ()))
    first_row = lax.dot_general(ones, first.astype(jnp.float32), turn, preferred_element_type=jnp.float32)
    second_row = lax.dot_general(ones, second.astype(jnp.float32), turn, preferred_element_type=jnp.float32)
    last_row = jnp.sum(jnp.where((row == flat) & valid, middle * share + place, 0), axis=0, keepdims=True)
    out_ref[...] = jnp.zeros(out_ref.shape, jnp.int32)
    out_ref[0:1, 0:held] = first_row[0:1].astype(jnp.int32)
    out_ref[1:2, 0:held] = second_row[0:1].astype(jnp.int32)
    out_ref[2:3, :] = last_row
    out_ref[3:4, :] = jnp.broadcast_to(most.astype(jnp.int32), (1, LANES))


def find_routes(page_table, groups, peers, held, share):
    padded = jnp.broadcast_to(jnp.pad(page_table, ((0, 0), (0, LANES - held))), (8, LANES))
    total = groups * peers
    return pl.pallas_call(
        functools.partial(route_kernel, groups, peers, held, share),
        out_shape=jax.ShapeDtypeStruct((8, LANES), jnp.int32),
        in_specs=[pl.BlockSpec(memory_space=pltpu.VMEM)],
        out_specs=pl.BlockSpec(memory_space=pltpu.VMEM),
        scratch_shapes=[
            pltpu.VMEM((total, 8, LANES), jnp.int32),
            pltpu.SemaphoreType.DMA((total,)),
            pltpu.SemaphoreType.DMA((total,)),
        ],
        compiler_params=pltpu.CompilerParams(collective_id=0, has_side_effects=True),
        name="routes",
    )(padded)


def hops_kernel(
    peers, held, share, route_ref, store_ref, out_ref, *scratch
):
    out1, in1, out2, in2 = scratch[0:2], scratch[2:4], scratch[4:6], scratch[6:8]
    s1, r1, s2, r2 = scratch[8:12]
    group = lax.axis_index("groups")
    me = lax.axis_index("replica")
    half = store_ref.shape[2] // 2
    barrier = pltpu.get_barrier_semaphore()

    def peer(step):
        return lax.rem(me + step, peers)

    def greet(step, carry):
        pl.semaphore_signal(barrier, inc=1, device_id=(group, peer(step)), device_id_type=MESH)
        return carry

    lax.fori_loop(1, peers, greet, 0)

    def block(index):
        return pl.ds(index * share, share)

    def copy(part, step, source, target, send_sem, recv_sem, who):
        other = peer(step)
        return pltpu.make_async_remote_copy(
            src_ref=source[part].at[block(other)],
            dst_ref=target[part].at[block(who)],
            send_sem=send_sem.at[part, step],
            recv_sem=recv_sem.at[part, who],
            device_id=(group, other),
            device_id_type=MESH,
        )

    def start_all(part, source, target, send_sem, recv_sem):
        def one(step, carry):
            copy(part, step, source, target, send_sem, recv_sem, me).start()
            return carry

        lax.fori_loop(1, peers, one, 0)
        target[part][block(me)] = source[part][block(me)]

    def await_all(part, source, target, send_sem, recv_sem):
        def one(step, carry):
            copy(part, step, source, target, send_sem, recv_sem, peer(step)).wait_recv()
            return carry

        lax.fori_loop(1, peers, one, 0)

    def drain(part, source, target, send_sem, recv_sem):
        def one(step, carry):
            copy(part, step, source, target, send_sem, recv_sem, me).wait_send()
            return carry

        lax.fori_loop(1, peers, one, 0)

    hop1 = (out1, in1, s1, r1)
    hop2 = (out2, in2, s2, r2)
    for part in range(2):
        columns = slice(part * half, (part + 1) * half)

        def gather(index, carry):
            out1[part][index] = store_ref[route_ref[0, index], :, columns]
            return carry

        lax.fori_loop(0, held, gather, 0)
        if part == 0:
            pl.semaphore_wait(barrier, peers - 1)
        start_all(part, *hop1)
    for part in range(2):
        await_all(part, *hop1)

        def forward(index, carry):
            out2[part][index] = in1[part][route_ref[1, index]]
            return carry

        lax.fori_loop(0, held, forward, 0)
        start_all(part, *hop2)
    for part in range(2):
        columns = slice(part * half, (part + 1) * half)
        await_all(part, *hop2)

        def settle(index, carry):
            upper = in2[part][route_ref[2, 2 * index]].astype(jnp.float32)
            lower = in2[part][route_ref[2, 2 * index + 1]].astype(jnp.float32)
            both = jnp.concatenate([upper, lower], axis=0).astype(out_ref.dtype)
            out_ref[pl.ds(pl.multiple_of(index * 16, 16), 16), columns] = both
            return carry

        lax.fori_loop(0, held // 2, settle, 0)
    for part in range(2):
        drain(part, *hop1)
        drain(part, *hop2)


def two_hops(routes, page_store, peers, held, share):
    page, width = page_store.shape[1:]
    buffer = pltpu.VMEM((held, page, width // 2), page_store.dtype)
    sems = pltpu.SemaphoreType.DMA((2, peers))
    return pl.pallas_call(
        functools.partial(hops_kernel, peers, held, share),
        out_shape=jax.ShapeDtypeStruct((held * page, width), page_store.dtype),
        in_specs=[
            pl.BlockSpec(memory_space=pltpu.SMEM),
            pl.BlockSpec(memory_space=pltpu.VMEM),
        ],
        out_specs=pl.BlockSpec(memory_space=pltpu.VMEM),
        scratch_shapes=[buffer] * 8 + [sems] * 4,
        compiler_params=pltpu.CompilerParams(
            collective_id=1, has_side_effects=True, vmem_limit_bytes=32 * 1024 * 1024
        ),
        name="hops",
    )(routes, page_store)


def attend_kernel(length_ref, cos_ref, sin_ref, q_ref, k_ref, v_ref, pk_ref, pv_ref, o_ref):
    gain = 50.0 * math.log2(math.e)
    shrink = HD ** (-0.5) / 50.0
    half = HD // 2
    heads = QH // KH
    cosine = cos_ref[...]
    sine = sin_ref[...]
    contract = (((1,), (1,)), ((), ()))

    def turn(values):
        leading = values[:, :half]
        trailing = values[:, half:]
        return jnp.concatenate(
            [leading * cosine - trailing * sine, trailing * cosine + leading * sine], axis=1
        )

    tokens = pk_ref.shape[0]
    column = lax.broadcasted_iota(jnp.int32, (1, tokens), 1)
    bias = jnp.where(column < length_ref[0], 0.0, -1e30).astype(jnp.float32)
    causal = lax.broadcasted_iota(jnp.int32, (CLEN, CLEN), 0) >= lax.broadcasted_iota(
        jnp.int32, (CLEN, CLEN), 1
    )
    pk = pk_ref[...]
    pv = pv_ref[...]
    span = 2 * CLEN
    for pair in range(q_ref.shape[0] // span):
        rows = slice(pair * span, (pair + 1) * span)
        queries = q_ref[rows, :].astype(jnp.float32)
        keys = k_ref[rows, :].astype(jnp.float32)
        values = v_ref[rows, :].astype(jnp.float32)
        results = []
        for cand in range(2):
            part = slice(cand * CLEN, (cand + 1) * CLEN)
            own_k = turn(keys[part]).astype(jnp.bfloat16)
            own_v = values[part].astype(jnp.bfloat16)
            row = []
            for head in range(heads):
                rotated = turn(queries[part, head * HD : (head + 1) * HD]).astype(jnp.bfloat16)
                far = lax.dot_general(rotated, pk, contract, preferred_element_type=jnp.float32)
                near = lax.dot_general(rotated, own_k, contract, preferred_element_type=jnp.float32)
                far = jnp.exp2(jnp.tanh(far * shrink) * gain + bias)
                near = jnp.where(causal, jnp.exp2(jnp.tanh(near * shrink) * gain), 0.0)
                total = jnp.sum(far, axis=1, keepdims=True) + jnp.sum(near, axis=1, keepdims=True)
                mixed = jnp.dot(far.astype(jnp.bfloat16), pv, preferred_element_type=jnp.float32)
                mixed = mixed + jnp.dot(
                    near.astype(jnp.bfloat16), own_v, preferred_element_type=jnp.float32
                )
                row.append(mixed / total)
            results.append(row)
        for head in range(heads):
            both = jnp.concatenate([results[0][head], results[1][head]], axis=0)
            o_ref[rows, head * HD : (head + 1) * HD] = both.astype(o_ref.dtype)


def attend(length, cosine, sine, queries, paired, prefix):
    rows = queries.shape[0]
    tokens = prefix.shape[0]
    wide = (QH // KH) * HD
    whole = lambda g: (0, 0)
    return pl.pallas_call(
        attend_kernel,
        grid=(KH,),
        out_shape=jax.ShapeDtypeStruct(queries.shape, queries.dtype),
        in_specs=[
            pl.BlockSpec(memory_space=pltpu.SMEM),
            pl.BlockSpec((CLEN, HD // 2), whole),
            pl.BlockSpec((CLEN, HD // 2), whole),
            pl.BlockSpec((rows, wide), lambda g: (0, g)),
            pl.BlockSpec((rows, HD), lambda g: (0, g)),
            pl.BlockSpec((rows, HD), lambda g: (0, KH + g)),
            pl.BlockSpec((tokens, HD), lambda g: (0, g)),
            pl.BlockSpec((tokens, HD), lambda g: (0, KH + g)),
        ],
        out_specs=pl.BlockSpec((rows, wide), lambda g: (0, g)),
        compiler_params=pltpu.CompilerParams(vmem_limit_bytes=48 * 1024 * 1024),
        name="attend",
    )(length, cosine, sine, queries, paired, paired, prefix, prefix)


def body(page_table, prefix_len, page_store, cand_query, cand_kv):
    groups = lax.axis_size("groups")
    peers = lax.axis_size("replica")
    held = page_store.shape[0]
    share = held // peers
    capacity = max(2, 4 * held // peers)
    length = prefix_len[0]
    positions = length + jnp.arange(CLEN, dtype=jnp.int32)
    pair_index = jnp.arange(HD // 2, dtype=jnp.float32)
    inverse = jnp.power(jnp.float32(10000.0), pair_index * (-2.0 / HD))
    angles = positions.astype(jnp.float32)[:, None] * inverse[None, :]
    cosine = jnp.cos(angles)
    sine = jnp.sin(angles)
    if share * peers == held and 2 * share < capacity:
        routes = find_routes(page_table, groups, peers, held, share)
        prefix = lax.cond(
            routes[3, 0] < share,
            lambda: two_hops(routes, page_store, peers, held, share),
            lambda: padded_exchange(page_table, page_store),
        )
    else:
        prefix = padded_exchange(page_table, page_store)
    return attend(prefix_len, cosine, sine, cand_query[0], cand_kv[0], prefix)[None]


def solution(mesh):
    return jax.shard_map(
        body,
        mesh=mesh,
        in_specs=(
            P(("groups", "replica"), None),
            P(("groups", "replica")),
            P(("groups", "replica"), None, None),
            P(("groups", "replica"), None, None),
            P(("groups", "replica"), None, None),
        ),
        out_specs=P(("groups", "replica"), None, None),
        check_vma=False,
    )
```

```python
import functools
import math

import jax
import jax.numpy as jnp
from jax import lax
from jax.experimental import pallas as pl
from jax.experimental.pallas import tpu as pltpu
from jax.sharding import PartitionSpec as P

HD = 256
QH = 8
KH = 4
CLEN = 200
LANES = 128
MESH = pl.DeviceIdType.MESH


def pick_slots(tables, chosen, capacity, held):
    counted = jnp.cumsum(chosen.astype(jnp.int32), axis=1) - 1
    picked = chosen[:, None, :] & (counted[:, None, :] == jnp.arange(capacity)[None, :, None])
    return jnp.sum(jnp.where(picked, (tables % held)[:, None, :], 0), axis=2)


def padded_exchange(page_table, page_store):
    peers = lax.axis_size("replica")
    my_index = lax.axis_index("replica")
    held = page_store.shape[0]
    capacity = max(2, 4 * held // peers)
    table = page_table[0]
    source = (table // held) % peers
    page_ids = jnp.arange(held)
    same_source = (source[:, None] == source[None, :]) & (page_ids[None, :] < page_ids[:, None])
    rank_here = jnp.sum(same_source.astype(jnp.int32), axis=1)
    every_table = lax.all_gather(page_table, "replica", axis=0, tiled=True)
    mine = (every_table // held) % peers == my_index
    send_slot = pick_slots(every_table, mine, capacity, held)
    outgoing = page_store[send_slot]
    arrived = lax.all_to_all(outgoing, "replica", split_axis=0, concat_axis=0, tiled=True)
    return arrived[source, rank_here].reshape(held * page_store.shape[1], page_store.shape[2])


def route_kernel(groups, peers, held, share, table_ref, out_ref, tables, send_sem, recv_sem):
    group = lax.axis_index("groups")
    me = lax.axis_index("replica")
    total = groups * peers
    flat = group * peers + me
    barrier = pltpu.get_barrier_semaphore()

    def where_is(step):
        other = lax.rem(flat + step, total)
        return other, (lax.div(other, peers), lax.rem(other, peers))

    def greet(step, carry):
        pl.semaphore_signal(barrier, inc=1, device_id=where_is(step)[1], device_id_type=MESH)
        return carry

    lax.fori_loop(1, total, greet, 0)
    tables[pl.ds(flat, 1)] = table_ref[...][None]
    pl.semaphore_wait(barrier, total - 1)

    def outgoing(step):
        return pltpu.make_async_remote_copy(
            src_ref=table_ref,
            dst_ref=tables.at[flat],
            send_sem=send_sem.at[step],
            recv_sem=recv_sem.at[flat],
            device_id=where_is(step)[1],
            device_id_type=MESH,
        )

    def send(step, carry):
        outgoing(step).start()
        return carry

    def finish(step, carry):
        other, place = where_is(step)
        pltpu.make_async_remote_copy(
            src_ref=table_ref,
            dst_ref=tables.at[other],
            send_sem=send_sem.at[step],
            recv_sem=recv_sem.at[other],
            device_id=place,
            device_id_type=MESH,
        ).wait()
        return carry

    lax.fori_loop(1, total, send, 0)
    lax.fori_loop(1, total, finish, 0)

    every = tables[:, 0, :]
    shape = (total, LANES)
    row = lax.broadcasted_iota(jnp.int32, shape, 0)
    lane = lax.broadcasted_iota(jnp.int32, shape, 1)
    valid = lane < held
    query = lax.rem(row, peers)
    owner = jnp.where(valid, lax.rem(lax.div(every, held), peers), -1)
    slot = lax.rem(every, held)
    before = (
        lax.broadcasted_iota(jnp.int32, (LANES, LANES), 0)
        < lax.broadcasted_iota(jnp.int32, (LANES, LANES), 1)
    ).astype(jnp.float32)
    left = lax.broadcasted_iota(jnp.int32, (total, total), 0)
    right = lax.broadcasted_iota(jnp.int32, (total, total), 1)
    together = lax.div(left, peers) == lax.div(right, peers)
    rank = jnp.zeros(shape, jnp.float32)
    for device in range(peers):
        here = (owner == device).astype(jnp.float32)
        along = jnp.dot(here, before, preferred_element_type=jnp.float32)
        nearer = lax.rem(right + (peers - device), peers) < lax.rem(left + (peers - device), peers)
        earlier = (together & nearer).astype(jnp.float32)
        above = jnp.dot(earlier, here, preferred_element_type=jnp.float32)
        above = jnp.sum(above, axis=1, keepdims=True)
        rank = rank + here * (along + above)
    rank = rank.astype(jnp.int32)
    middle = jnp.where(valid, lax.rem(rank, peers), -1)
    layer = lax.div(rank, peers)
    place = jnp.zeros(shape, jnp.float32)
    for device in range(peers):
        here = (middle == device).astype(jnp.float32)
        along = jnp.dot(here, before, preferred_element_type=jnp.float32)
        place = place + here * along
    most = jnp.max(jnp.max(place, axis=1, keepdims=True), axis=0, keepdims=True)
    place = place.astype(jnp.int32)

    mine = lax.div(row, peers) == group
    first_key = jnp.where(mine & (owner == me), middle * share + layer, -1)
    second_key = jnp.where(mine & (middle == me), query * share + place, -1)
    second_value = owner * share + layer
    spots = lax.broadcasted_iota(jnp.int32, (held, LANES), 0)
    first = jnp.zeros((held, LANES), jnp.int32)
    second = jnp.zeros((held, LANES), jnp.int32)
    for index in range(total):
        cut = slice(index, index + 1)
        first = first + jnp.where(spots == first_key[cut], slot[cut], 0)
        second = second + jnp.where(spots == second_key[cut], second_value[cut], 0)
    ones = jnp.ones((8, LANES), jnp.float32)
    turn = (((1,), (1,)), ((), ()))
    first_row = lax.dot_general(ones, first.astype(jnp.float32), turn, preferred_element_type=jnp.float32)
    second_row = lax.dot_general(ones, second.astype(jnp.float32), turn, preferred_element_type=jnp.float32)
    last_row = jnp.sum(jnp.where((row == flat) & valid, middle * share + place, 0), axis=0, keepdims=True)
    out_ref[...] = jnp.zeros(out_ref.shape, jnp.int32)
    out_ref[0:1, 0:held] = first_row[0:1].astype(jnp.int32)
    out_ref[1:2, 0:held] = second_row[0:1].astype(jnp.int32)
    out_ref[2:3, :] = last_row
    out_ref[3:4, :] = jnp.broadcast_to(most.astype(jnp.int32), (1, LANES))


def find_routes(page_table, groups, peers, held, share):
    padded = jnp.broadcast_to(jnp.pad(page_table, ((0, 0), (0, LANES - held))), (8, LANES))
    total = groups * peers
    return pl.pallas_call(
        functools.partial(route_kernel, groups, peers, held, share),
        out_shape=jax.ShapeDtypeStruct((8, LANES), jnp.int32),
        in_specs=[pl.BlockSpec(memory_space=pltpu.VMEM)],
        out_specs=pl.BlockSpec(memory_space=pltpu.VMEM),
        scratch_shapes=[
            pltpu.VMEM((total, 8, LANES), jnp.int32),
            pltpu.SemaphoreType.DMA((total,)),
            pltpu.SemaphoreType.DMA((total,)),
        ],
        compiler_params=pltpu.CompilerParams(collective_id=0, has_side_effects=True),
        name="routes",
    )(padded)


def serve_kernel(
    peers, held, share, route_ref, length_ref, cos_ref, sin_ref, store_ref, q_ref, kv_ref, o_ref, *scratch
):
    out1, in1, out2, in2 = (scratch[i * KH : (i + 1) * KH] for i in range(4))
    s1, r1, s2, r2, prefix = scratch[4 * KH :]
    group = lax.axis_index("groups")
    me = lax.axis_index("replica")
    barrier = pltpu.get_barrier_semaphore()

    def peer(step):
        return lax.rem(me + step, peers)

    def greet(step, carry):
        pl.semaphore_signal(barrier, inc=1, device_id=(group, peer(step)), device_id_type=MESH)
        return carry

    lax.fori_loop(1, peers, greet, 0)

    def block(index):
        return pl.ds(index * share, share)

    def copy(part, step, source, target, send_sem, recv_sem, who):
        other = peer(step)
        return pltpu.make_async_remote_copy(
            src_ref=source[part].at[block(other)],
            dst_ref=target[part].at[block(who)],
            send_sem=send_sem.at[part, step],
            recv_sem=recv_sem.at[part, who],
            device_id=(group, other),
            device_id_type=MESH,
        )

    def start_all(part, source, target, send_sem, recv_sem):
        def one(step, carry):
            copy(part, step, source, target, send_sem, recv_sem, me).start()
            return carry

        lax.fori_loop(1, peers, one, 0)
        target[part][block(me)] = source[part][block(me)]

    def await_all(part, source, target, send_sem, recv_sem):
        def one(step, carry):
            copy(part, step, source, target, send_sem, recv_sem, peer(step)).wait_recv()
            return carry

        lax.fori_loop(1, peers, one, 0)

    def drain(part, source, target, send_sem, recv_sem):
        def one(step, carry):
            copy(part, step, source, target, send_sem, recv_sem, me).wait_send()
            return carry

        lax.fori_loop(1, peers, one, 0)

    hop1 = (out1, in1, s1, r1)
    hop2 = (out2, in2, s2, r2)
    for part in range(KH):
        key_columns = slice(part * HD, (part + 1) * HD)
        value_columns = slice((KH + part) * HD, (KH + part + 1) * HD)

        def gather(index, carry):
            out1[part][index, :, 0:HD] = store_ref[route_ref[0, index], :, key_columns]
            out1[part][index, :, HD:] = store_ref[route_ref[0, index], :, value_columns]
            return carry

        lax.fori_loop(0, held, gather, 0)
        if part == 0:
            pl.semaphore_wait(barrier, peers - 1)
        start_all(part, *hop1)
    for part in range(KH):
        await_all(part, *hop1)

        def forward(index, carry):
            out2[part][index] = in1[part][route_ref[1, index]]
            return carry

        lax.fori_loop(0, held, forward, 0)
        start_all(part, *hop2)
    for part in range(KH):
        await_all(part, *hop2)

        def settle(index, carry):
            upper = in2[part][route_ref[2, 2 * index]].astype(jnp.float32)
            lower = in2[part][route_ref[2, 2 * index + 1]].astype(jnp.float32)
            both = jnp.concatenate([upper, lower], axis=0).astype(prefix.dtype)
            prefix[pl.ds(pl.multiple_of(index * 16, 16), 16), :] = both
            return carry

        lax.fori_loop(0, held // 2, settle, 0)
        wide = (QH // KH) * HD
        attend_head(
            length_ref,
            cos_ref,
            sin_ref,
            q_ref.at[:, part * wide : (part + 1) * wide],
            kv_ref.at[:, part * HD : (part + 1) * HD],
            kv_ref.at[:, (KH + part) * HD : (KH + part + 1) * HD],
            prefix[:, 0:HD],
            prefix[:, HD:],
            o_ref.at[:, part * wide : (part + 1) * wide],
        )
    for part in range(KH):
        drain(part, *hop1)
        drain(part, *hop2)


def serve(routes, length, cosine, sine, page_store, queries, paired, peers, held, share):
    page = page_store.shape[1]
    buffer = pltpu.VMEM((held, page, 2 * HD), page_store.dtype)
    sems = pltpu.SemaphoreType.DMA((KH, peers))
    vmem = pl.BlockSpec(memory_space=pltpu.VMEM)
    smem = pl.BlockSpec(memory_space=pltpu.SMEM)
    return pl.pallas_call(
        functools.partial(serve_kernel, peers, held, share),
        out_shape=jax.ShapeDtypeStruct(queries.shape, queries.dtype),
        in_specs=[smem, smem, vmem, vmem, vmem, vmem, vmem],
        out_specs=vmem,
        scratch_shapes=[buffer] * (4 * KH)
        + [sems] * 4
        + [pltpu.VMEM((held * page, 2 * HD), page_store.dtype)],
        compiler_params=pltpu.CompilerParams(
            collective_id=1, has_side_effects=True, vmem_limit_bytes=48 * 1024 * 1024
        ),
        name="serve",
    )(routes, length, cosine, sine, page_store, queries, paired)


def attend_head(length_ref, cos_ref, sin_ref, q_ref, k_ref, v_ref, pk, pv, o_ref):
    gain = 50.0 * math.log2(math.e)
    shrink = HD ** (-0.5) / 50.0
    half = HD // 2
    heads = QH // KH
    cosine = cos_ref[...]
    sine = sin_ref[...]
    contract = (((1,), (1,)), ((), ()))

    def turn(values):
        leading = values[:, :half]
        trailing = values[:, half:]
        return jnp.concatenate(
            [leading * cosine - trailing * sine, trailing * cosine + leading * sine], axis=1
        )

    tokens = pk.shape[0]
    column = lax.broadcasted_iota(jnp.int32, (1, tokens), 1)
    bias = jnp.where(column < length_ref[0], 0.0, -1e30).astype(jnp.float32)
    causal = lax.broadcasted_iota(jnp.int32, (CLEN, CLEN), 0) >= lax.broadcasted_iota(
        jnp.int32, (CLEN, CLEN), 1
    )
    span = 2 * CLEN

    def one_pair(pair, carry):
        rows = pl.ds(pl.multiple_of(pair * span, span), span)
        queries = q_ref[rows, :].astype(jnp.float32)
        keys = k_ref[rows, :].astype(jnp.float32)
        values = v_ref[rows, :].astype(jnp.float32)
        results = []
        for cand in range(2):
            part = slice(cand * CLEN, (cand + 1) * CLEN)
            own_k = turn(keys[part]).astype(jnp.bfloat16)
            own_v = values[part].astype(jnp.bfloat16)
            row = []
            for head in range(heads):
                rotated = turn(queries[part, head * HD : (head + 1) * HD]).astype(jnp.bfloat16)
                far = lax.dot_general(rotated, pk, contract, preferred_element_type=jnp.float32)
                near = lax.dot_general(rotated, own_k, contract, preferred_element_type=jnp.float32)
                far = jnp.exp2(jnp.tanh(far * shrink) * gain + bias)
                near = jnp.where(causal, jnp.exp2(jnp.tanh(near * shrink) * gain), 0.0)
                total = jnp.sum(far, axis=1, keepdims=True) + jnp.sum(near, axis=1, keepdims=True)
                mixed = jnp.dot(far.astype(jnp.bfloat16), pv, preferred_element_type=jnp.float32)
                mixed = mixed + jnp.dot(
                    near.astype(jnp.bfloat16), own_v, preferred_element_type=jnp.float32
                )
                row.append(mixed / total)
            results.append(row)
        for head in range(heads):
            both = jnp.concatenate([results[0][head], results[1][head]], axis=0)
            o_ref[rows, head * HD : (head + 1) * HD] = both.astype(o_ref.dtype)
        return carry

    lax.fori_loop(0, q_ref.shape[0] // span, one_pair, 0)


def attend_kernel(length_ref, cos_ref, sin_ref, q_ref, k_ref, v_ref, pk_ref, pv_ref, o_ref):
    attend_head(length_ref, cos_ref, sin_ref, q_ref, k_ref, v_ref, pk_ref[...], pv_ref[...], o_ref)


def attend(length, cosine, sine, queries, paired, prefix):
    rows = queries.shape[0]
    tokens = prefix.shape[0]
    wide = (QH // KH) * HD
    whole = lambda g: (0, 0)
    return pl.pallas_call(
        attend_kernel,
        grid=(KH,),
        out_shape=jax.ShapeDtypeStruct(queries.shape, queries.dtype),
        in_specs=[
            pl.BlockSpec(memory_space=pltpu.SMEM),
            pl.BlockSpec((CLEN, HD // 2), whole),
            pl.BlockSpec((CLEN, HD // 2), whole),
            pl.BlockSpec((rows, wide), lambda g: (0, g)),
            pl.BlockSpec((rows, HD), lambda g: (0, g)),
            pl.BlockSpec((rows, HD), lambda g: (0, KH + g)),
            pl.BlockSpec((tokens, HD), lambda g: (0, g)),
            pl.BlockSpec((tokens, HD), lambda g: (0, KH + g)),
        ],
        out_specs=pl.BlockSpec((rows, wide), lambda g: (0, g)),
        compiler_params=pltpu.CompilerParams(vmem_limit_bytes=48 * 1024 * 1024),
        name="attend",
    )(length, cosine, sine, queries, paired, paired, prefix, prefix)


def body(page_table, prefix_len, page_store, cand_query, cand_kv):
    groups = lax.axis_size("groups")
    peers = lax.axis_size("replica")
    held = page_store.shape[0]
    share = held // peers
    capacity = max(2, 4 * held // peers)
    length = prefix_len[0]
    positions = length + jnp.arange(CLEN, dtype=jnp.int32)
    pair_index = jnp.arange(HD // 2, dtype=jnp.float32)
    inverse = jnp.power(jnp.float32(10000.0), pair_index * (-2.0 / HD))
    angles = positions.astype(jnp.float32)[:, None] * inverse[None, :]
    cosine = jnp.cos(angles)
    sine = jnp.sin(angles)
    queries = cand_query[0]
    paired = cand_kv[0]

    def padded():
        prefix = padded_exchange(page_table, page_store)
        return attend(prefix_len, cosine, sine, queries, paired, prefix)

    def hopped():
        return serve(
            routes, prefix_len, cosine, sine, page_store, queries, paired, peers, held, share
        )

    if share * peers == held and 2 * share < capacity:
        routes = find_routes(page_table, groups, peers, held, share)
        return lax.cond(routes[3, 0] < share, hopped, padded)[None]
    return padded()[None]


def solution(mesh):
    return jax.shard_map(
        body,
        mesh=mesh,
        in_specs=(
            P(("groups", "replica"), None),
            P(("groups", "replica")),
            P(("groups", "replica"), None, None),
            P(("groups", "replica"), None, None),
            P(("groups", "replica"), None, None),
        ),
        out_specs=P(("groups", "replica"), None, None),
        check_vma=False,
    )
```

```python
import functools
import math

import jax
import jax.numpy as jnp
from jax import lax
from jax.experimental import pallas as pl
from jax.experimental.pallas import tpu as pltpu
from jax.sharding import PartitionSpec as P

HD = 256
QH = 8
KH = 4
CLEN = 200
LANES = 128
MESH = pl.DeviceIdType.MESH


def pick_slots(tables, chosen, capacity, held):
    counted = jnp.cumsum(chosen.astype(jnp.int32), axis=1) - 1
    picked = chosen[:, None, :] & (counted[:, None, :] == jnp.arange(capacity)[None, :, None])
    return jnp.sum(jnp.where(picked, (tables % held)[:, None, :], 0), axis=2)


def padded_exchange(page_table, page_store):
    peers = lax.axis_size("replica")
    my_index = lax.axis_index("replica")
    held = page_store.shape[0]
    capacity = max(2, 4 * held // peers)
    table = page_table[0]
    source = (table // held) % peers
    page_ids = jnp.arange(held)
    same_source = (source[:, None] == source[None, :]) & (page_ids[None, :] < page_ids[:, None])
    rank_here = jnp.sum(same_source.astype(jnp.int32), axis=1)
    every_table = lax.all_gather(page_table, "replica", axis=0, tiled=True)
    mine = (every_table // held) % peers == my_index
    send_slot = pick_slots(every_table, mine, capacity, held)
    outgoing = page_store[send_slot]
    arrived = lax.all_to_all(outgoing, "replica", split_axis=0, concat_axis=0, tiled=True)
    return arrived[source, rank_here].reshape(held * page_store.shape[1], page_store.shape[2])


def split(values, size):
    if size & (size - 1) == 0:
        return lax.shift_right_logical(values, jnp.int32(size.bit_length() - 1)), values & (size - 1)
    return lax.div(values, size), lax.rem(values, size)


def route_kernel(groups, peers, held, share, row_ref, out_ref, most_ref, table_ref, tables, send_sem, recv_sem):
    group = lax.axis_index("groups")
    me = lax.axis_index("replica")
    total = groups * peers
    flat = group * peers + me
    barrier = pltpu.get_barrier_semaphore()

    def where_is(step):
        other = lax.rem(flat + step, total)
        return other, (lax.div(other, peers), lax.rem(other, peers))

    def greet(step, carry):
        pl.semaphore_signal(barrier, inc=1, device_id=where_is(step)[1], device_id_type=MESH)
        return carry

    lax.fori_loop(1, total, greet, 0)
    table_ref[...] = jnp.zeros(table_ref.shape, jnp.int32)
    table_ref[0:1, 0:held] = row_ref[...]
    tables[pl.ds(flat, 1)] = table_ref[...][None]
    pl.semaphore_wait(barrier, total - 1)

    def outgoing(step):
        return pltpu.make_async_remote_copy(
            src_ref=table_ref,
            dst_ref=tables.at[flat],
            send_sem=send_sem.at[step],
            recv_sem=recv_sem.at[flat],
            device_id=where_is(step)[1],
            device_id_type=MESH,
        )

    def send(step, carry):
        outgoing(step).start()
        return carry

    def finish(step, carry):
        other, place = where_is(step)
        pltpu.make_async_remote_copy(
            src_ref=table_ref,
            dst_ref=tables.at[other],
            send_sem=send_sem.at[step],
            recv_sem=recv_sem.at[other],
            device_id=place,
            device_id_type=MESH,
        ).wait()
        return carry

    lax.fori_loop(1, total, send, 0)
    lax.fori_loop(1, total, finish, 0)

    every = tables[:, 0, :]
    shape = (total, LANES)
    row = lax.broadcasted_iota(jnp.int32, shape, 0)
    lane = lax.broadcasted_iota(jnp.int32, shape, 1)
    valid = lane < held
    query = row
    for lap in range(1, groups):
        query = jnp.where(row >= lap * peers, row - lap * peers, query)
    device_of, slot = split(every, held)
    owner = jnp.where(valid, split(device_of, peers)[1], -1)
    before = (
        lax.broadcasted_iota(jnp.int32, (LANES, LANES), 0)
        < lax.broadcasted_iota(jnp.int32, (LANES, LANES), 1)
    ).astype(jnp.float32)
    left = lax.broadcasted_iota(jnp.int32, (total, total), 0)
    right = lax.broadcasted_iota(jnp.int32, (total, total), 1)
    left_lap, left = split(left, peers)
    right_lap, right = split(right, peers)
    together = left_lap == right_lap
    rank = jnp.zeros(shape, jnp.float32)
    for device in range(peers):
        here = (owner == device).astype(jnp.float32)
        along = jnp.dot(here, before, preferred_element_type=jnp.float32)
        nearer = jnp.where(right < device, right + peers, right) < jnp.where(
            left < device, left + peers, left
        )
        earlier = (together & nearer).astype(jnp.float32)
        above = jnp.dot(earlier, here, preferred_element_type=jnp.float32)
        above = jnp.sum(above, axis=1, keepdims=True)
        rank = rank + here * (along + above)
    rank = rank.astype(jnp.int32)
    layer, middle = split(rank, peers)
    middle = jnp.where(valid, middle, -1)
    place = jnp.zeros(shape, jnp.float32)
    for device in range(peers):
        here = (middle == device).astype(jnp.float32)
        along = jnp.dot(here, before, preferred_element_type=jnp.float32)
        place = place + here * along
    most = jnp.max(jnp.max(place, axis=1, keepdims=True), axis=0, keepdims=True)
    place = place.astype(jnp.int32)

    mine = (row >= group * peers) & (row < (group + 1) * peers)
    first_key = jnp.where(mine & (owner == me), middle * share + layer, -1)
    second_key = jnp.where(mine & (middle == me), query * share + place, -1)
    second_value = owner * share + layer
    spots = lax.broadcasted_iota(jnp.int32, (held, LANES), 0)
    first = jnp.zeros((held, LANES), jnp.int32)
    second = jnp.zeros((held, LANES), jnp.int32)
    for index in range(total):
        cut = slice(index, index + 1)
        first = first + jnp.where(spots == first_key[cut], slot[cut], 0)
        second = second + jnp.where(spots == second_key[cut], second_value[cut], 0)
    ones = jnp.ones((8, LANES), jnp.float32)
    turn = (((1,), (1,)), ((), ()))
    first_row = lax.dot_general(ones, first.astype(jnp.float32), turn, preferred_element_type=jnp.float32)
    second_row = lax.dot_general(ones, second.astype(jnp.float32), turn, preferred_element_type=jnp.float32)
    last_row = jnp.sum(jnp.where((row == flat) & valid, middle * share + place, 0), axis=0, keepdims=True)
    out_ref[...] = jnp.zeros(out_ref.shape, jnp.int32)
    out_ref[0:1, 0:held] = first_row[0:1].astype(jnp.int32)
    out_ref[1:2, 0:held] = second_row[0:1].astype(jnp.int32)
    out_ref[2:3, :] = last_row
    most_ref[...] = most.astype(jnp.int32)


def find_routes(page_table, groups, peers, held, share):
    total = groups * peers
    return pl.pallas_call(
        functools.partial(route_kernel, groups, peers, held, share),
        out_shape=[
            jax.ShapeDtypeStruct((8, LANES), jnp.int32),
            jax.ShapeDtypeStruct((1, 1), jnp.int32),
        ],
        in_specs=[pl.BlockSpec(memory_space=pltpu.VMEM)],
        out_specs=[pl.BlockSpec(memory_space=pltpu.VMEM)] * 2,
        scratch_shapes=[
            pltpu.VMEM((8, LANES), jnp.int32),
            pltpu.VMEM((total, 8, LANES), jnp.int32),
            pltpu.SemaphoreType.DMA((total,)),
            pltpu.SemaphoreType.DMA((total,)),
        ],
        compiler_params=pltpu.CompilerParams(collective_id=0, has_side_effects=True),
        name="routes",
    )(page_table)


def serve_kernel(
    peers, held, share, route_ref, length_ref, cos_ref, sin_ref, store_ref, q_ref, kv_ref, o_ref, *scratch
):
    out1, in1, out2, in2 = (scratch[i * KH : (i + 1) * KH] for i in range(4))
    s1, r1, s2, r2, prefix = scratch[4 * KH :]
    group = lax.axis_index("groups")
    me = lax.axis_index("replica")
    barrier = pltpu.get_barrier_semaphore()

    def peer(step):
        return lax.rem(me + step, peers)

    def greet(step, carry):
        pl.semaphore_signal(barrier, inc=1, device_id=(group, peer(step)), device_id_type=MESH)
        return carry

    lax.fori_loop(1, peers, greet, 0)

    def block(index):
        return pl.ds(index * share, share)

    def copy(part, step, source, target, send_sem, recv_sem, who):
        other = peer(step)
        return pltpu.make_async_remote_copy(
            src_ref=source[part].at[block(other)],
            dst_ref=target[part].at[block(who)],
            send_sem=send_sem.at[part, step],
            recv_sem=recv_sem.at[part, who],
            device_id=(group, other),
            device_id_type=MESH,
        )

    def start_all(part, source, target, send_sem, recv_sem):
        def one(step, carry):
            copy(part, step, source, target, send_sem, recv_sem, me).start()
            return carry

        lax.fori_loop(1, peers, one, 0)
        target[part][block(me)] = source[part][block(me)]

    def await_all(part, source, target, send_sem, recv_sem):
        def one(step, carry):
            copy(part, step, source, target, send_sem, recv_sem, peer(step)).wait_recv()
            return carry

        lax.fori_loop(1, peers, one, 0)

    def drain(part, source, target, send_sem, recv_sem):
        def one(step, carry):
            copy(part, step, source, target, send_sem, recv_sem, me).wait_send()
            return carry

        lax.fori_loop(1, peers, one, 0)

    hop1 = (out1, in1, s1, r1)
    hop2 = (out2, in2, s2, r2)
    for part in range(KH):
        key_columns = slice(part * HD, (part + 1) * HD)
        value_columns = slice((KH + part) * HD, (KH + part + 1) * HD)

        def gather(index, carry):
            out1[part][index, :, 0:HD] = store_ref[route_ref[0, index], :, key_columns]
            out1[part][index, :, HD:] = store_ref[route_ref[0, index], :, value_columns]
            return carry

        lax.fori_loop(0, held, gather, 0)
        if part == 0:
            pl.semaphore_wait(barrier, peers - 1)
        start_all(part, *hop1)
    for part in range(KH):
        await_all(part, *hop1)

        def forward(index, carry):
            out2[part][index] = in1[part][route_ref[1, index]]
            return carry

        lax.fori_loop(0, held, forward, 0)
        start_all(part, *hop2)
    for part in range(KH):
        await_all(part, *hop2)

        def settle(index, carry):
            upper = in2[part][route_ref[2, 2 * index]].astype(jnp.float32)
            lower = in2[part][route_ref[2, 2 * index + 1]].astype(jnp.float32)
            both = jnp.concatenate([upper, lower], axis=0).astype(prefix.dtype)
            prefix[pl.ds(pl.multiple_of(index * 16, 16), 16), :] = both
            return carry

        lax.fori_loop(0, held // 2, settle, 0)
        wide = (QH // KH) * HD
        attend_head(
            length_ref,
            cos_ref,
            sin_ref,
            q_ref.at[:, part * wide : (part + 1) * wide],
            kv_ref.at[:, part * HD : (part + 1) * HD],
            kv_ref.at[:, (KH + part) * HD : (KH + part + 1) * HD],
            prefix[:, 0:HD],
            prefix[:, HD:],
            o_ref.at[:, part * wide : (part + 1) * wide],
        )
    for part in range(KH):
        drain(part, *hop1)
        drain(part, *hop2)


def serve(routes, length, cosine, sine, page_store, queries, paired, peers, held, share):
    page = page_store.shape[1]
    buffer = pltpu.VMEM((held, page, 2 * HD), page_store.dtype)
    sems = pltpu.SemaphoreType.DMA((KH, peers))
    vmem = pl.BlockSpec(memory_space=pltpu.VMEM)
    smem = pl.BlockSpec(memory_space=pltpu.SMEM)
    return pl.pallas_call(
        functools.partial(serve_kernel, peers, held, share),
        out_shape=jax.ShapeDtypeStruct(queries.shape, queries.dtype),
        in_specs=[smem, smem, vmem, vmem, vmem, vmem, vmem],
        out_specs=vmem,
        scratch_shapes=[buffer] * (4 * KH)
        + [sems] * 4
        + [pltpu.VMEM((held * page, 2 * HD), page_store.dtype)],
        compiler_params=pltpu.CompilerParams(
            collective_id=1, has_side_effects=True, vmem_limit_bytes=48 * 1024 * 1024
        ),
        name="serve",
    )(routes, length, cosine, sine, page_store, queries, paired)


def attend_head(length_ref, cos_ref, sin_ref, q_ref, k_ref, v_ref, pk, pv, o_ref):
    gain = 50.0 * math.log2(math.e)
    shrink = HD ** (-0.5) / 50.0
    half = HD // 2
    heads = QH // KH
    cosine = cos_ref[...]
    sine = sin_ref[...]
    contract = (((1,), (1,)), ((), ()))

    def turn(values):
        leading = values[:, :half]
        trailing = values[:, half:]
        return jnp.concatenate(
            [leading * cosine - trailing * sine, trailing * cosine + leading * sine], axis=1
        )

    tokens = pk.shape[0]
    column = lax.broadcasted_iota(jnp.int32, (1, tokens), 1)
    bias = jnp.where(column < length_ref[0], 0.0, -1e30).astype(jnp.float32)
    causal = lax.broadcasted_iota(jnp.int32, (CLEN, CLEN), 0) >= lax.broadcasted_iota(
        jnp.int32, (CLEN, CLEN), 1
    )
    span = 2 * CLEN

    def one_pair(pair, carry):
        rows = pl.ds(pl.multiple_of(pair * span, span), span)
        queries = q_ref[rows, :].astype(jnp.float32)
        keys = k_ref[rows, :].astype(jnp.float32)
        values = v_ref[rows, :].astype(jnp.float32)
        results = []
        for cand in range(2):
            part = slice(cand * CLEN, (cand + 1) * CLEN)
            own_k = turn(keys[part]).astype(jnp.bfloat16)
            own_v = values[part].astype(jnp.bfloat16)
            row = []
            for head in range(heads):
                rotated = turn(queries[part, head * HD : (head + 1) * HD]).astype(jnp.bfloat16)
                far = lax.dot_general(rotated, pk, contract, preferred_element_type=jnp.float32)
                near = lax.dot_general(rotated, own_k, contract, preferred_element_type=jnp.float32)
                far = jnp.exp2(jnp.tanh(far * shrink) * gain + bias)
                near = jnp.where(causal, jnp.exp2(jnp.tanh(near * shrink) * gain), 0.0)
                total = jnp.sum(far, axis=1, keepdims=True) + jnp.sum(near, axis=1, keepdims=True)
                mixed = jnp.dot(far.astype(jnp.bfloat16), pv, preferred_element_type=jnp.float32)
                mixed = mixed + jnp.dot(
                    near.astype(jnp.bfloat16), own_v, preferred_element_type=jnp.float32
                )
                row.append(mixed / total)
            results.append(row)
        for head in range(heads):
            both = jnp.concatenate([results[0][head], results[1][head]], axis=0)
            o_ref[rows, head * HD : (head + 1) * HD] = both.astype(o_ref.dtype)
        return carry

    lax.fori_loop(0, q_ref.shape[0] // span, one_pair, 0)


def attend_kernel(length_ref, cos_ref, sin_ref, q_ref, k_ref, v_ref, pk_ref, pv_ref, o_ref):
    attend_head(length_ref, cos_ref, sin_ref, q_ref, k_ref, v_ref, pk_ref[...], pv_ref[...], o_ref)


def attend(length, cosine, sine, queries, paired, prefix):
    rows = queries.shape[0]
    tokens = prefix.shape[0]
    wide = (QH // KH) * HD
    whole = lambda g: (0, 0)
    return pl.pallas_call(
        attend_kernel,
        grid=(KH,),
        out_shape=jax.ShapeDtypeStruct(queries.shape, queries.dtype),
        in_specs=[
            pl.BlockSpec(memory_space=pltpu.SMEM),
            pl.BlockSpec((CLEN, HD // 2), whole),
            pl.BlockSpec((CLEN, HD // 2), whole),
            pl.BlockSpec((rows, wide), lambda g: (0, g)),
            pl.BlockSpec((rows, HD), lambda g: (0, g)),
            pl.BlockSpec((rows, HD), lambda g: (0, KH + g)),
            pl.BlockSpec((tokens, HD), lambda g: (0, g)),
            pl.BlockSpec((tokens, HD), lambda g: (0, KH + g)),
        ],
        out_specs=pl.BlockSpec((rows, wide), lambda g: (0, g)),
        compiler_params=pltpu.CompilerParams(vmem_limit_bytes=48 * 1024 * 1024),
        name="attend",
    )(length, cosine, sine, queries, paired, paired, prefix, prefix)


def body(page_table, prefix_len, page_store, cand_query, cand_kv):
    groups = lax.axis_size("groups")
    peers = lax.axis_size("replica")
    held = page_store.shape[0]
    share = held // peers
    capacity = max(2, 4 * held // peers)
    length = prefix_len[0]
    positions = length + jnp.arange(CLEN, dtype=jnp.int32)
    pair_index = jnp.arange(HD // 2, dtype=jnp.float32)
    inverse = jnp.power(jnp.float32(10000.0), pair_index * (-2.0 / HD))
    angles = positions.astype(jnp.float32)[:, None] * inverse[None, :]
    cosine = jnp.cos(angles)
    sine = jnp.sin(angles)
    queries = cand_query[0]
    paired = cand_kv[0]

    def padded():
        prefix = padded_exchange(page_table, page_store)
        return attend(prefix_len, cosine, sine, queries, paired, prefix)

    def hopped():
        return serve(
            routes, prefix_len, cosine, sine, page_store, queries, paired, peers, held, share
        )

    if share * peers == held and 2 * share < capacity:
        routes, most = find_routes(page_table, groups, peers, held, share)
        return lax.cond(most[0, 0] < share, hopped, padded)[None]
    return padded()[None]


def solution(mesh):
    return jax.shard_map(
        body,
        mesh=mesh,
        in_specs=(
            P(("groups", "replica"), None),
            P(("groups", "replica")),
            P(("groups", "replica"), None, None),
            P(("groups", "replica"), None, None),
            P(("groups", "replica"), None, None),
        ),
        out_specs=P(("groups", "replica"), None, None),
        check_vma=False,
    )
```

```python
import functools
import math

import jax
import jax.numpy as jnp
from jax import lax
from jax.experimental import pallas as pl
from jax.experimental.pallas import tpu as pltpu
from jax.sharding import PartitionSpec as P

HD = 256
QH = 8
KH = 4
CLEN = 200
LANES = 128
MESH = pl.DeviceIdType.MESH


def pick_slots(tables, chosen, capacity, held):
    counted = jnp.cumsum(chosen.astype(jnp.int32), axis=1) - 1
    picked = chosen[:, None, :] & (counted[:, None, :] == jnp.arange(capacity)[None, :, None])
    return jnp.sum(jnp.where(picked, (tables % held)[:, None, :], 0), axis=2)


def padded_exchange(page_table, page_store):
    peers = lax.axis_size("replica")
    my_index = lax.axis_index("replica")
    held = page_store.shape[0]
    capacity = max(2, 4 * held // peers)
    table = page_table[0]
    source = (table // held) % peers
    page_ids = jnp.arange(held)
    same_source = (source[:, None] == source[None, :]) & (page_ids[None, :] < page_ids[:, None])
    rank_here = jnp.sum(same_source.astype(jnp.int32), axis=1)
    every_table = lax.all_gather(page_table, "replica", axis=0, tiled=True)
    mine = (every_table // held) % peers == my_index
    send_slot = pick_slots(every_table, mine, capacity, held)
    outgoing = page_store[send_slot]
    arrived = lax.all_to_all(outgoing, "replica", split_axis=0, concat_axis=0, tiled=True)
    return arrived[source, rank_here].reshape(held * page_store.shape[1], page_store.shape[2])


def split(values, size):
    if size & (size - 1) == 0:
        return lax.shift_right_logical(values, jnp.int32(size.bit_length() - 1)), values & (size - 1)
    return lax.div(values, size), lax.rem(values, size)


def route_kernel(groups, peers, held, share, row_ref, out_ref, most_ref, table_ref, tables, send_sem, recv_sem):
    group = lax.axis_index("groups")
    me = lax.axis_index("replica")
    total = groups * peers
    flat = group * peers + me
    barrier = pltpu.get_barrier_semaphore()

    def where_is(step):
        other = lax.rem(flat + step, total)
        return other, (lax.div(other, peers), lax.rem(other, peers))

    def greet(step, carry):
        pl.semaphore_signal(barrier, inc=1, device_id=where_is(step)[1], device_id_type=MESH)
        return carry

    lax.fori_loop(1, total, greet, 0)
    table_ref[...] = jnp.zeros(table_ref.shape, jnp.int32)
    table_ref[0:1, 0:held] = row_ref[...]
    tables[pl.ds(flat, 1)] = table_ref[...][None]
    pl.semaphore_wait(barrier, total - 1)

    def outgoing(step):
        return pltpu.make_async_remote_copy(
            src_ref=table_ref,
            dst_ref=tables.at[flat],
            send_sem=send_sem.at[step],
            recv_sem=recv_sem.at[flat],
            device_id=where_is(step)[1],
            device_id_type=MESH,
        )

    def send(step, carry):
        outgoing(step).start()
        return carry

    def finish(step, carry):
        other, place = where_is(step)
        pltpu.make_async_remote_copy(
            src_ref=table_ref,
            dst_ref=tables.at[other],
            send_sem=send_sem.at[step],
            recv_sem=recv_sem.at[other],
            device_id=place,
            device_id_type=MESH,
        ).wait()
        return carry

    lax.fori_loop(1, total, send, 0)
    lax.fori_loop(1, total, finish, 0)

    every = tables[:, 0, :]
    shape = (total, LANES)
    row = lax.broadcasted_iota(jnp.int32, shape, 0)
    lane = lax.broadcasted_iota(jnp.int32, shape, 1)
    valid = lane < held
    query = row
    for lap in range(1, groups):
        query = jnp.where(row >= lap * peers, row - lap * peers, query)
    device_of, slot = split(every, held)
    owner = jnp.where(valid, split(device_of, peers)[1], -1)
    before = (
        lax.broadcasted_iota(jnp.int32, (LANES, LANES), 0)
        < lax.broadcasted_iota(jnp.int32, (LANES, LANES), 1)
    ).astype(jnp.float32)
    left = lax.broadcasted_iota(jnp.int32, (total, total), 0)
    right = lax.broadcasted_iota(jnp.int32, (total, total), 1)
    left_lap, left = split(left, peers)
    right_lap, right = split(right, peers)
    together = left_lap == right_lap
    spans = [slice(device * total, (device + 1) * total) for device in range(peers)]
    here = [(owner == device).astype(jnp.float32) for device in range(peers)]
    along = jnp.dot(jnp.concatenate(here, axis=0), before, preferred_element_type=jnp.float32)
    counts = jnp.zeros(shape, jnp.float32)
    earlier = []
    for device in range(peers):
        counts = jnp.where(lane == device, jnp.sum(here[device], axis=1, keepdims=True), counts)
        nearer = jnp.where(right < device, right + peers, right) < jnp.where(
            left < device, left + peers, left
        )
        earlier.append((together & nearer).astype(jnp.float32))
    above = jnp.dot(jnp.concatenate(earlier, axis=0), counts, preferred_element_type=jnp.float32)
    rank = jnp.zeros(shape, jnp.float32)
    for device in range(peers):
        ahead = jnp.where(lane == device, above[spans[device]], 0.0)
        ahead = jnp.sum(ahead, axis=1, keepdims=True)
        rank = rank + here[device] * (along[spans[device]] + ahead)
    rank = rank.astype(jnp.int32)
    layer, middle = split(rank, peers)
    middle = jnp.where(valid, middle, -1)
    here = [(middle == device).astype(jnp.float32) for device in range(peers)]
    along = jnp.dot(jnp.concatenate(here, axis=0), before, preferred_element_type=jnp.float32)
    place = jnp.zeros(shape, jnp.float32)
    for device in range(peers):
        place = place + here[device] * along[spans[device]]
    most = jnp.max(jnp.max(place, axis=1, keepdims=True), axis=0, keepdims=True)
    place = place.astype(jnp.int32)

    mine = (row >= group * peers) & (row < (group + 1) * peers)
    first_key = jnp.where(mine & (owner == me), middle * share + layer, -1)
    second_key = jnp.where(mine & (middle == me), query * share + place, -1)
    second_value = owner * share + layer
    spots = lax.broadcasted_iota(jnp.int32, (held, LANES), 0)
    first = jnp.zeros((held, LANES), jnp.int32)
    second = jnp.zeros((held, LANES), jnp.int32)
    for index in range(total):
        cut = slice(index, index + 1)
        first = first + jnp.where(spots == first_key[cut], slot[cut], 0)
        second = second + jnp.where(spots == second_key[cut], second_value[cut], 0)
    ones = jnp.ones((8, LANES), jnp.float32)
    turn = (((1,), (1,)), ((), ()))
    first_row = lax.dot_general(ones, first.astype(jnp.float32), turn, preferred_element_type=jnp.float32)
    second_row = lax.dot_general(ones, second.astype(jnp.float32), turn, preferred_element_type=jnp.float32)
    last_row = jnp.sum(jnp.where((row == flat) & valid, middle * share + place, 0), axis=0, keepdims=True)
    out_ref[...] = jnp.zeros(out_ref.shape, jnp.int32)
    out_ref[0:1, 0:held] = first_row[0:1].astype(jnp.int32)
    out_ref[1:2, 0:held] = second_row[0:1].astype(jnp.int32)
    out_ref[2:3, :] = last_row
    most_ref[...] = most.astype(jnp.int32)


def find_routes(page_table, groups, peers, held, share):
    total = groups * peers
    return pl.pallas_call(
        functools.partial(route_kernel, groups, peers, held, share),
        out_shape=[
            jax.ShapeDtypeStruct((8, LANES), jnp.int32),
            jax.ShapeDtypeStruct((1, 1), jnp.int32),
        ],
        in_specs=[pl.BlockSpec(memory_space=pltpu.VMEM)],
        out_specs=[pl.BlockSpec(memory_space=pltpu.VMEM)] * 2,
        scratch_shapes=[
            pltpu.VMEM((8, LANES), jnp.int32),
            pltpu.VMEM((total, 8, LANES), jnp.int32),
            pltpu.SemaphoreType.DMA((total,)),
            pltpu.SemaphoreType.DMA((total,)),
        ],
        compiler_params=pltpu.CompilerParams(collective_id=0, has_side_effects=True),
        name="routes",
    )(page_table)


def serve_kernel(
    peers, held, share, route_ref, length_ref, cos_ref, sin_ref, store_ref, q_ref, kv_ref, o_ref, *scratch
):
    out1, in1, out2, in2 = (scratch[i * KH : (i + 1) * KH] for i in range(4))
    s1, r1, s2, r2, prefix = scratch[4 * KH :]
    group = lax.axis_index("groups")
    me = lax.axis_index("replica")
    barrier = pltpu.get_barrier_semaphore()

    def peer(step):
        return lax.rem(me + step, peers)

    def greet(step, carry):
        pl.semaphore_signal(barrier, inc=1, device_id=(group, peer(step)), device_id_type=MESH)
        return carry

    lax.fori_loop(1, peers, greet, 0)

    def block(index):
        return pl.ds(index * share, share)

    def copy(part, step, source, target, send_sem, recv_sem, who):
        other = peer(step)
        return pltpu.make_async_remote_copy(
            src_ref=source[part].at[block(other)],
            dst_ref=target[part].at[block(who)],
            send_sem=send_sem.at[part, step],
            recv_sem=recv_sem.at[part, who],
            device_id=(group, other),
            device_id_type=MESH,
        )

    def start_all(part, source, target, send_sem, recv_sem):
        def one(step, carry):
            copy(part, step, source, target, send_sem, recv_sem, me).start()
            return carry

        lax.fori_loop(1, peers, one, 0)
        target[part][block(me)] = source[part][block(me)]

    def await_all(part, source, target, send_sem, recv_sem):
        def one(step, carry):
            copy(part, step, source, target, send_sem, recv_sem, peer(step)).wait_recv()
            return carry

        lax.fori_loop(1, peers, one, 0)

    def drain(part, source, target, send_sem, recv_sem):
        def one(step, carry):
            copy(part, step, source, target, send_sem, recv_sem, me).wait_send()
            return carry

        lax.fori_loop(1, peers, one, 0)

    hop1 = (out1, in1, s1, r1)
    hop2 = (out2, in2, s2, r2)
    for part in range(KH):
        key_columns = slice(part * HD, (part + 1) * HD)
        value_columns = slice((KH + part) * HD, (KH + part + 1) * HD)

        def gather(index, carry):
            out1[part][index, :, 0:HD] = store_ref[route_ref[0, index], :, key_columns]
            out1[part][index, :, HD:] = store_ref[route_ref[0, index], :, value_columns]
            return carry

        lax.fori_loop(0, held, gather, 0)
        if part == 0:
            pl.semaphore_wait(barrier, peers - 1)
        start_all(part, *hop1)
    for part in range(KH):
        await_all(part, *hop1)

        def forward(index, carry):
            out2[part][index] = in1[part][route_ref[1, index]]
            return carry

        lax.fori_loop(0, held, forward, 0)
        start_all(part, *hop2)
    for part in range(KH):
        await_all(part, *hop2)

        def settle(index, carry):
            upper = in2[part][route_ref[2, 2 * index]].astype(jnp.float32)
            lower = in2[part][route_ref[2, 2 * index + 1]].astype(jnp.float32)
            both = jnp.concatenate([upper, lower], axis=0).astype(prefix.dtype)
            prefix[pl.ds(pl.multiple_of(index * 16, 16), 16), :] = both
            return carry

        lax.fori_loop(0, held // 2, settle, 0)
        wide = (QH // KH) * HD
        attend_head(
            length_ref,
            cos_ref,
            sin_ref,
            q_ref.at[:, part * wide : (part + 1) * wide],
            kv_ref.at[:, part * HD : (part + 1) * HD],
            kv_ref.at[:, (KH + part) * HD : (KH + part + 1) * HD],
            prefix[:, 0:HD],
            prefix[:, HD:],
            o_ref.at[:, part * wide : (part + 1) * wide],
        )
    for part in range(KH):
        drain(part, *hop1)
        drain(part, *hop2)


def serve(routes, length, cosine, sine, page_store, queries, paired, peers, held, share):
    page = page_store.shape[1]
    buffer = pltpu.VMEM((held, page, 2 * HD), page_store.dtype)
    sems = pltpu.SemaphoreType.DMA((KH, peers))
    vmem = pl.BlockSpec(memory_space=pltpu.VMEM)
    smem = pl.BlockSpec(memory_space=pltpu.SMEM)
    return pl.pallas_call(
        functools.partial(serve_kernel, peers, held, share),
        out_shape=jax.ShapeDtypeStruct(queries.shape, queries.dtype),
        in_specs=[smem, smem, vmem, vmem, vmem, vmem, vmem],
        out_specs=vmem,
        scratch_shapes=[buffer] * (4 * KH)
        + [sems] * 4
        + [pltpu.VMEM((held * page, 2 * HD), page_store.dtype)],
        compiler_params=pltpu.CompilerParams(
            collective_id=1, has_side_effects=True, vmem_limit_bytes=48 * 1024 * 1024
        ),
        name="serve",
    )(routes, length, cosine, sine, page_store, queries, paired)


def attend_head(length_ref, cos_ref, sin_ref, q_ref, k_ref, v_ref, pk, pv, o_ref):
    gain = 50.0 * math.log2(math.e)
    shrink = HD ** (-0.5) / 50.0
    half = HD // 2
    heads = QH // KH
    cosine = cos_ref[...]
    sine = sin_ref[...]
    contract = (((1,), (1,)), ((), ()))

    def turn(values):
        leading = values[:, :half]
        trailing = values[:, half:]
        return jnp.concatenate(
            [leading * cosine - trailing * sine, trailing * cosine + leading * sine], axis=1
        )

    tokens = pk.shape[0]
    column = lax.broadcasted_iota(jnp.int32, (1, tokens), 1)
    bias = jnp.where(column < length_ref[0], 0.0, -1e30).astype(jnp.float32)
    causal = lax.broadcasted_iota(jnp.int32, (CLEN, CLEN), 0) >= lax.broadcasted_iota(
        jnp.int32, (CLEN, CLEN), 1
    )
    span = 2 * CLEN

    def one_pair(pair, carry):
        rows = pl.ds(pl.multiple_of(pair * span, span), span)
        queries = q_ref[rows, :].astype(jnp.float32)
        keys = k_ref[rows, :].astype(jnp.float32)
        values = v_ref[rows, :].astype(jnp.float32)
        results = []
        for cand in range(2):
            part = slice(cand * CLEN, (cand + 1) * CLEN)
            own_k = turn(keys[part]).astype(jnp.bfloat16)
            own_v = values[part].astype(jnp.bfloat16)
            row = []
            for head in range(heads):
                rotated = turn(queries[part, head * HD : (head + 1) * HD]).astype(jnp.bfloat16)
                far = lax.dot_general(rotated, pk, contract, preferred_element_type=jnp.float32)
                near = lax.dot_general(rotated, own_k, contract, preferred_element_type=jnp.float32)
                far = jnp.exp2(jnp.tanh(far * shrink) * gain + bias)
                near = jnp.where(causal, jnp.exp2(jnp.tanh(near * shrink) * gain), 0.0)
                total = jnp.sum(far, axis=1, keepdims=True) + jnp.sum(near, axis=1, keepdims=True)
                mixed = jnp.dot(far.astype(jnp.bfloat16), pv, preferred_element_type=jnp.float32)
                mixed = mixed + jnp.dot(
                    near.astype(jnp.bfloat16), own_v, preferred_element_type=jnp.float32
                )
                row.append(mixed / total)
            results.append(row)
        for head in range(heads):
            both = jnp.concatenate([results[0][head], results[1][head]], axis=0)
            o_ref[rows, head * HD : (head + 1) * HD] = both.astype(o_ref.dtype)
        return carry

    lax.fori_loop(0, q_ref.shape[0] // span, one_pair, 0)


def attend_kernel(length_ref, cos_ref, sin_ref, q_ref, k_ref, v_ref, pk_ref, pv_ref, o_ref):
    attend_head(length_ref, cos_ref, sin_ref, q_ref, k_ref, v_ref, pk_ref[...], pv_ref[...], o_ref)


def attend(length, cosine, sine, queries, paired, prefix):
    rows = queries.shape[0]
    tokens = prefix.shape[0]
    wide = (QH // KH) * HD
    whole = lambda g: (0, 0)
    return pl.pallas_call(
        attend_kernel,
        grid=(KH,),
        out_shape=jax.ShapeDtypeStruct(queries.shape, queries.dtype),
        in_specs=[
            pl.BlockSpec(memory_space=pltpu.SMEM),
            pl.BlockSpec((CLEN, HD // 2), whole),
            pl.BlockSpec((CLEN, HD // 2), whole),
            pl.BlockSpec((rows, wide), lambda g: (0, g)),
            pl.BlockSpec((rows, HD), lambda g: (0, g)),
            pl.BlockSpec((rows, HD), lambda g: (0, KH + g)),
            pl.BlockSpec((tokens, HD), lambda g: (0, g)),
            pl.BlockSpec((tokens, HD), lambda g: (0, KH + g)),
        ],
        out_specs=pl.BlockSpec((rows, wide), lambda g: (0, g)),
        compiler_params=pltpu.CompilerParams(vmem_limit_bytes=48 * 1024 * 1024),
        name="attend",
    )(length, cosine, sine, queries, paired, paired, prefix, prefix)


def body(page_table, prefix_len, page_store, cand_query, cand_kv):
    groups = lax.axis_size("groups")
    peers = lax.axis_size("replica")
    held = page_store.shape[0]
    share = held // peers
    capacity = max(2, 4 * held // peers)
    length = prefix_len[0]
    positions = length + jnp.arange(CLEN, dtype=jnp.int32)
    pair_index = jnp.arange(HD // 2, dtype=jnp.float32)
    inverse = jnp.power(jnp.float32(10000.0), pair_index * (-2.0 / HD))
    angles = positions.astype(jnp.float32)[:, None] * inverse[None, :]
    cosine = jnp.cos(angles)
    sine = jnp.sin(angles)
    queries = cand_query[0]
    paired = cand_kv[0]

    def padded():
        prefix = padded_exchange(page_table, page_store)
        return attend(prefix_len, cosine, sine, queries, paired, prefix)

    def hopped():
        return serve(
            routes, prefix_len, cosine, sine, page_store, queries, paired, peers, held, share
        )

    if share * peers == held and 2 * share < capacity:
        routes, most = find_routes(page_table, groups, peers, held, share)
        return lax.cond(most[0, 0] < share, hopped, padded)[None]
    return padded()[None]


def solution(mesh):
    return jax.shard_map(
        body,
        mesh=mesh,
        in_specs=(
            P(("groups", "replica"), None),
            P(("groups", "replica")),
            P(("groups", "replica"), None, None),
            P(("groups", "replica"), None, None),
            P(("groups", "replica"), None, None),
        ),
        out_specs=P(("groups", "replica"), None, None),
        check_vma=False,
    )
```
